512 devices in a mesh: dp: 4 (over x), ctx: 32 (over y, z_lo), tensor: 4 (over z_hi, core).
Axes of the slice: x: 4, y: 4, z: 16 (z_hi: 2, z_lo: 8; z = z_hi * 8 + z_lo), core: 2. Of those that a mesh axis runs over, the one named last changes fastest.
Arguments:
- queries: bfloat16 [4, 4096, 2048], P('dp', 'ctx', 'tensor'), may hold values from -64 to 64
- neighbours: bfloat16 [4, 64, 256, 896], P('dp', 'ctx'), may hold values from -64 to 64
- key_weight: bfloat16 [896, 2048], P(None, 'tensor'), may hold values from -1 to 1
- value_weight: bfloat16 [896, 2048], P(None, 'tensor'), may hold values from -0.1875 to 0.1875
- neighbour_ids: int32 [4, 64, 256], P('dp', 'ctx'), may hold values from 0 to 127999, as said below
- block_document: int32 [4, 64], P('dp', 'ctx'), may hold values from 0 to 7, never falling along the last dimension, each value on 1 to 16 neighbouring positions
- grad_out: bfloat16 [4, 4096, 2048], P('dp', 'ctx', 'tensor'), may hold values from -6 to 6
Outputs:
- attended: bfloat16 [4, 4096, 2048], P('dp', 'ctx', 'tensor')
- grad_queries: bfloat16 [4, 4096, 2048], P('dp', 'ctx', 'tensor')
- grad_neighbours: bfloat16 [4, 64, 256, 896], P('dp', 'ctx')
- grad_key_weight: float32 [896, 2048], P(('dp', 'ctx'), 'tensor')
- grad_value_weight: float32 [896, 2048], P(('dp', 'ctx'), 'tensor')
The draws below stay inside these ranges and needn't reach their ends.
Inputs may be any that keep to these rules, and one draw needn't show every extreme that they name: `neighbour_ids`: id 0 marks a padding token; in each of the 2 neighbours of 128 tokens the padding tokens follow all real ones, and the first quarter of the 128 tokens is real. `block_document`: the document numbers of a sequence's stretches never fall.
All inputs are finite; a program needn't handle non-finite values.
Results may differ from the reference program's by a relative error of at most 0.015.
The reference program's roundings to bfloat16 on the way count: a program that leaves them out, or rounds other values in their place, can miss the bound.
Values may be sent and summed in bfloat16 or wider, within the bound.
No kernel may reach another device: no remote copies, remote signals or barrier semaphores. Data moves between devices by JAX's collectives and lax.ppermute only.
A program may use at most 64 MiB of HBM per device.

```python
import math
import jax
import jax.numpy as jnp
import numpy as np
from jax import lax

HEAD_DIM = 128
ENC = 896
VOCAB = 128000
HEADS = 16
STRETCH = 64
NEIGH = 2
NLEN = 128
SEQS = 4
SEQ_LEN = 4096
NCH = 64
CH_DEV = 2
KEYS = 256
WIDTH = 2048
SEQ_DEVS = 128


def shared_key_weight(key):
    drawn = jax.random.normal(jax.random.fold_in(key, 100), (ENC, WIDTH), jnp.float32) * ENC ** (-0.5)
    drawn = jnp.clip(drawn, -1.0, 1.0)
    return drawn.astype(jnp.bfloat16).astype(jnp.float32)


def draw_key_weight(key, part):
    return shared_key_weight(key).astype(jnp.bfloat16)


def draw_neighbours(key, part):
    key = jax.random.fold_in(key, 2)
    subkeys = jax.random.split(key, 2)
    drawn = jax.random.normal(subkeys[0], (SEQS, NCH, KEYS, ENC), jnp.float32)
    owner = (jnp.arange(SEQS)[:, None] * NCH + jnp.arange(NCH)[None, :]) // CH_DEV
    pairing = jax.random.permutation(subkeys[1], SEQ_DEVS)
    target = pairing[owner]
    feature_block = jnp.arange(ENC) // (ENC // SEQ_DEVS)
    boost = jnp.where(target[:, :, None, None] == feature_block[None, None, None, :], 4.0, 1.0)
    drawn = drawn * boost
    return jnp.clip(drawn, -64.0, 64.0).astype(jnp.bfloat16)


def draw_queries(key, part):
    key = jax.random.fold_in(key, 3)
    drawn = jax.random.normal(key, (SEQS, NCH, STRETCH, HEADS, HEAD_DIM), jnp.float32)
    return jnp.clip(drawn, -64.0, 64.0).reshape(SEQS, SEQ_LEN, WIDTH).astype(jnp.bfloat16)


def draw_neighbour_ids(key, part):
    key = jax.random.fold_in(key, 4)
    subkeys = jax.random.split(key, 2)
    lengths = jax.random.randint(subkeys[0], (SEQS, NCH, NEIGH, 1), NLEN // 4, NLEN + 1)
    tokens = jax.random.randint(subkeys[1], (SEQS, NCH, NEIGH, NLEN), 1, VOCAB)
    filled = jnp.where(jnp.arange(NLEN)[None, None, None, :] < lengths, tokens, 0)
    return filled.reshape(SEQS, NCH, KEYS).astype(jnp.int32)


def block_levels(own_key, dims, shards, least, largest):
    def one(dim, shards_of):
        draws = jax.random.uniform(jax.random.fold_in(jax.random.fold_in(own_key, 6), dim), (shards_of,), jnp.float32, least / len(shards), largest / len(shards))
        return jnp.repeat(jnp.exp(draws), dims[dim] // shards_of).reshape((-1,) + (1,) * (len(dims) - dim - 1))

    loudness = one(*shards[0])
    for cut in shards[1:]:
        loudness = loudness * one(*cut)
    return loudness


def length_profile(amount, total, reach, slope):
    weights = [(1 << 20) // math.isqrt(standing ** slope) + 1 for standing in range(2, amount + 1)]
    rest, counts = total - reach - (amount - 1), [1] * (amount - 1)
    while rest > 0:
        candidates = [i for i in range(amount - 1) if counts[i] < reach]
        pool, left = sum([weights[i] for i in candidates]), rest
        for i in candidates:
            more = min(reach - counts[i], max(1, left * weights[i] // pool), rest)
            counts[i] = counts[i] + more
            rest = rest - more
    return np.array([reach] + counts)


def ragged(rng, number_of, total, limit, lean):
    if number_of == 2:
        one = jax.random.randint(rng, (), max(1, total - limit), min(limit, total - 1) + 1)
        return jnp.stack([one, total - one])
    sizes = jnp.asarray(length_profile(number_of, total, limit, lean), jnp.int32)
    twos = (number_of - 1) // 2
    donor, sink = sizes[1:1 + 2 * twos:2], sizes[2:2 + 2 * twos:2]
    margin = jnp.minimum(donor - 1, limit - sink)
    moved = jax.random.randint(jax.random.fold_in(rng, 1), (twos,), 0, 1 << 20) % (margin + 1)
    sizes = sizes.at[1:1 + 2 * twos:2].set(donor - moved).at[2:2 + 2 * twos:2].set(sink + moved)
    return sizes[jax.random.permutation(jax.random.fold_in(rng, 2), number_of)]


def noise(own_key, extent, spread, reach, shards=(), held_as=jnp.bfloat16):
    entries = spread * jax.random.normal(own_key, extent, jnp.float32)
    if shards:
        entries = entries * block_levels(own_key, extent, shards, -0.22, 0.18)
    return jnp.clip(entries, -reach, reach).astype(held_as)


def setup_inputs(seed: int = 0) -> dict:
    keys = jax.random.split(jax.random.key(seed), 8)
    return {
        "queries": draw_queries(jax.random.fold_in(keys[7], 71), 0),
        "neighbours": draw_neighbours(jax.random.fold_in(keys[7], 71), 0),
        "key_weight": draw_key_weight(jax.random.fold_in(keys[7], 71), 0),
        "value_weight": noise(keys[3], (ENC, WIDTH), ENC ** -0.5, 0.1875, ((1, 4),)),
        "neighbour_ids": draw_neighbour_ids(jax.random.fold_in(keys[7], 71), 0),
        "block_document": jax.vmap(lambda own: jnp.searchsorted(jnp.cumsum(ragged(own, max(2, NCH // 8), NCH, max(2, NCH // 4), 0)), jnp.arange(NCH), side="right"))(jax.random.split(keys[5], SEQS)).reshape((SEQS, NCH)).astype(jnp.int32),
        "grad_out": noise(keys[6], (SEQS, SEQ_LEN, WIDTH), 1.0, 6.0, ((0, 4), (1, 32), (2, 4))),
    }


masked_score = -1.0e30


def block_attention(query_blocks, source_keys, source_values, source_ids, block_gate, grad_blocks):
    score_scale = HEAD_DIM ** -0.5
    scores = jnp.einsum("cthd,cjhd->chtj", query_blocks.astype(jnp.float32), source_keys.astype(jnp.float32)) * score_scale
    usable = (source_ids != 0)[:, None, None, :]
    scores = jnp.where(usable, scores, masked_score)
    row_max = jnp.max(scores, axis=-1, keepdims=True)
    raised = jnp.exp(scores - row_max)
    weights = raised / jnp.sum(raised, axis=-1, keepdims=True)
    weights_half = weights.astype(jnp.bfloat16)
    gate_rows = block_gate[:, None, None, None]
    mixed = jnp.einsum("chtj,cjhd->cthd", weights_half.astype(jnp.float32), source_values.astype(jnp.float32)) * gate_rows
    attended = mixed.astype(jnp.bfloat16)
    gated_grad = jnp.where(gate_rows > 0, grad_blocks, jnp.zeros_like(grad_blocks))
    grad_weights = jnp.einsum("cthd,cjhd->chtj", gated_grad.astype(jnp.float32), source_values.astype(jnp.float32))
    inner = jnp.sum(weights * grad_weights, axis=-1, keepdims=True)
    grad_scores = (weights * (grad_weights - inner) * score_scale).astype(jnp.bfloat16)
    grad_queries = jnp.einsum("chtj,cjhd->cthd", grad_scores.astype(jnp.float32), source_keys.astype(jnp.float32)).astype(jnp.bfloat16)
    grad_keys = jnp.einsum("chtj,cthd->cjhd", grad_scores.astype(jnp.float32), query_blocks.astype(jnp.float32)).astype(jnp.bfloat16)
    grad_values = jnp.einsum("chtj,cthd->cjhd", weights_half.astype(jnp.float32), gated_grad.astype(jnp.float32)).astype(jnp.bfloat16)
    return attended, grad_queries, grad_keys, grad_values


def per_sequence(members):
    return block_attention(members[0], members[1], members[2], members[3], members[4], members[5])


def reference(queries, neighbours, key_weight, value_weight, neighbour_ids, block_document, grad_out):
    flat_rows = neighbours.reshape(SEQS * NCH * KEYS, ENC)
    keys_all = jnp.dot(flat_rows, key_weight, preferred_element_type=jnp.float32).astype(jnp.bfloat16).reshape(SEQS, NCH, KEYS, HEADS, HEAD_DIM)
    values_all = jnp.dot(flat_rows, value_weight, preferred_element_type=jnp.float32).astype(jnp.bfloat16).reshape(SEQS, NCH, KEYS, HEADS, HEAD_DIM)
    source_keys = jnp.concatenate([jnp.zeros_like(keys_all[:, :1]), keys_all[:, :-1]], axis=1)
    source_values = jnp.concatenate([jnp.zeros_like(values_all[:, :1]), values_all[:, :-1]], axis=1)
    source_ids = jnp.concatenate([jnp.zeros_like(neighbour_ids[:, :1]), neighbour_ids[:, :-1]], axis=1)
    previous = jnp.concatenate([jnp.full((SEQS, 1), -1, jnp.int32), block_document[:, :-1]], axis=1)
    block_gate = (block_document == previous).astype(jnp.float32)
    query_blocks = queries.reshape(SEQS, NCH, STRETCH, HEADS, HEAD_DIM)
    grad_blocks = grad_out.reshape(SEQS, NCH, STRETCH, HEADS, HEAD_DIM)
    attended, grad_queries, grad_keys, grad_values = lax.map(per_sequence, (query_blocks, source_keys, source_values, source_ids, block_gate, grad_blocks))
    owned_keys = jnp.concatenate([grad_keys[:, 1:], jnp.zeros_like(grad_keys[:, :1])], axis=1).reshape(SEQS * NCH * KEYS, WIDTH)
    owned_values = jnp.concatenate([grad_values[:, 1:], jnp.zeros_like(grad_values[:, :1])], axis=1).reshape(SEQS * NCH * KEYS, WIDTH)
    grad_rows = jnp.dot(owned_keys, key_weight.T, preferred_element_type=jnp.float32) + jnp.dot(owned_values, value_weight.T, preferred_element_type=jnp.float32)
    grad_neighbours = grad_rows.astype(jnp.bfloat16).reshape(SEQS, NCH, KEYS, ENC)
    grad_key_weight = jnp.dot(flat_rows.T, owned_keys, preferred_element_type=jnp.float32)
    grad_value_weight = jnp.dot(flat_rows.T, owned_values, preferred_element_type=jnp.float32)
    return (attended.reshape(SEQS, SEQ_LEN, WIDTH), grad_queries.reshape(SEQS, SEQ_LEN, WIDTH), grad_neighbours, grad_key_weight, grad_value_weight)
```

```python
import functools

import jax
import jax.numpy as jnp
import numpy as np
from jax import lax
from jax.experimental import pallas as pl
from jax.experimental.pallas import tpu as pltpu
from jax.sharding import Mesh, PartitionSpec as P

HEAD_DIM = 128
STRETCH = 64
BF16 = jnp.bfloat16
F32 = jnp.float32

masked_score = -1e30


def matmul(left, right, left_dim, right_dim):
    contracted = (((left_dim,), (right_dim,)), ((), ()))
    return lax.dot_general(left, right, contracted, preferred_element_type=F32)


def attend(encodings, key_weight, value_weight, usable, gate, queries, grad_out, out):
    attended, grad_queries, grad_keys, grad_values = out
    score_scale = HEAD_DIM ** (-0.5)
    keys_all = matmul(encodings, key_weight[...], 1, 0).astype(BF16)
    values_all = matmul(encodings, value_weight[...], 1, 0).astype(BF16)
    gated_all = jnp.where(gate, grad_out, jnp.zeros_like(grad_out))
    for head in range(queries.shape[1] // HEAD_DIM):
        span = slice(head * HEAD_DIM, (head + 1) * HEAD_DIM)
        query, grad = queries[:, span], gated_all[:, span]
        keys, values = keys_all[:, span], values_all[:, span]
        scores = jnp.where(usable, matmul(query, keys, 1, 1) * score_scale, masked_score)
        raised = jnp.exp(scores - jnp.max(scores, axis=-1, keepdims=True))
        weights = raised / jnp.sum(raised, axis=-1, keepdims=True)
        weights_half = weights.astype(BF16)
        mixed = matmul(weights_half, values, 1, 0)
        attended[:, span] = jnp.where(gate, mixed, 0.0).astype(BF16)
        grad_weights = matmul(grad, values, 1, 1)
        inner = jnp.sum(weights * grad_weights, axis=-1, keepdims=True)
        grad_scores = (weights * (grad_weights - inner) * score_scale).astype(BF16)
        grad_queries[:, span] = matmul(grad_scores, keys, 1, 0).astype(BF16)
        grad_keys[:, span] = matmul(grad_scores, query, 0, 0).astype(BF16)
        grad_values[:, span] = matmul(weights_half, grad, 0, 0).astype(BF16)


def encoding_partials(core, key_weight, value_weight, grad_keys, grad_values, kept, sent):
    half = kept.shape[0]

    def partial_of(part):
        rows = pl.ds(pl.multiple_of(part * half, half), half)
        return matmul(grad_keys[rows, :], key_weight[...], 1, 1) + matmul(
            grad_values[rows, :], value_weight[...], 1, 1
        )

    sent[...] = partial_of(1 - core).astype(BF16)
    kept[...] = partial_of(core)


def own_pair(facts, neighbours, key_weight, value_weight, ids, queries, grad_out, *out):
    attended, grad_queries, grad_keys, grad_values, kept, sent = out
    gate = jnp.full((1, 1), facts[0], jnp.int32) == facts[1]
    attend(
        neighbours[0], key_weight, value_weight, ids[0:1, :] != 0, gate,
        queries[STRETCH:, :], grad_out[STRETCH:, :],
        (attended, grad_queries, grad_keys, grad_values),
    )
    encoding_partials(facts[2], key_weight, value_weight, grad_keys, grad_values, kept, sent)


def next_pair(facts, neighbours, key_weight, value_weight, ids, payload, first_keys, first_values, *out):
    answer, kept, sent, weight_grad, grad_keys, grad_values = out
    document = payload[2 * STRETCH:2 * STRETCH + 1, 0:1].astype(F32)
    follows = jnp.full((1, 1), facts[3], jnp.int32) == 1
    gate = jnp.logical_and(document == facts[1].astype(F32), follows)
    attend(
        neighbours[1], key_weight, value_weight, ids[1:2, :] != 0, gate,
        payload[0:STRETCH, :], payload[STRETCH:2 * STRETCH, :],
        (answer.at[0:STRETCH], answer.at[STRETCH:2 * STRETCH], grad_keys, grad_values),
    )
    encoding_partials(facts[2], key_weight, value_weight, grad_keys, grad_values, kept, sent)
    width = grad_keys.shape[1]
    for side, (first, second) in enumerate(((first_keys, grad_keys), (first_values, grad_values))):
        total = matmul(neighbours[0], first[...], 0, 0) + matmul(neighbours[1], second[...], 0, 0)
        weight_grad[:, side * width:(side + 1) * width] = total.astype(BF16)


def call(kernel, out_shapes, scratch, flops, moved):
    vmem = pl.BlockSpec(memory_space=pltpu.VMEM)
    smem = pl.BlockSpec(memory_space=pltpu.SMEM)

    def run(facts, *arrays):
        return pl.pallas_call(
            kernel,
            out_shape=[jax.ShapeDtypeStruct(s, d) for s, d in out_shapes],
            in_specs=[smem] + [vmem] * len(arrays),
            out_specs=[vmem] * len(out_shapes),
            scratch_shapes=[pltpu.VMEM(s, d) for s, d in scratch],
            compiler_params=pltpu.CompilerParams(vmem_limit_bytes=48 * 2**20),
            cost_estimate=pl.CostEstimate(flops=flops, bytes_accessed=moved, transcendentals=65536),
        )(facts, *arrays)

    return run


def swap(block, axis):
    return lax.ppermute(block, axis, [(0, 1), (1, 0)])


def shards(queries, neighbours, key_weight, value_weight, neighbour_ids, block_document, grad_out):
    tokens, width = queries.shape[1:]
    slots, enc_width = neighbours.shape[2:]
    half = slots // 2
    run_count = lax.axis_size("y") * lax.axis_size("z")
    run_index = lax.axis_index(("y", "z"))
    documents = block_document[0]
    facts = jnp.stack(
        [
            documents[0],
            documents[1],
            lax.axis_index("c").astype(jnp.int32),
            (run_index < run_count - 1).astype(jnp.int32),
        ]
    )
    document_rows = jnp.broadcast_to(documents[0].astype(BF16), (16, width))
    payload = jnp.concatenate(
        [queries[0, :STRETCH], grad_out[0, :STRETCH], document_rows], axis=0
    )
    payload = lax.ppermute(payload, ("y", "z"), [(i, i - 1) for i in range(1, run_count)])

    pair_out = [
        ((STRETCH, width), BF16),
        ((STRETCH, width), BF16),
        ((slots, width), BF16),
        ((slots, width), BF16),
        ((half, enc_width), F32),
        ((half, enc_width), BF16),
    ]
    attended, grad_queries, first_keys, first_values, kept_a, sent_a = call(
        own_pair, pair_out, [], 1_100_000_000, 4_000_000
    )(facts, neighbours[0], key_weight, value_weight, neighbour_ids[0], queries[0], grad_out[0])
    got_a = swap(sent_a, "c")

    next_out = [
        ((2 * STRETCH, width), BF16),
        ((half, enc_width), F32),
        ((half, enc_width), BF16),
        ((enc_width, 2 * width), BF16),
    ]
    answer, kept_b, sent_b, weight_grad = call(
        next_pair, next_out, [((slots, width), BF16)] * 2, 2_000_000_000, 6_000_000
    )(facts, neighbours[0], key_weight, value_weight, neighbour_ids[0], payload, first_keys, first_values)
    got_b = swap(sent_b, "c")

    chip_a = (kept_a + got_a.astype(F32)).astype(BF16)
    far_a = swap(chip_a, "h")
    chip_b = (kept_b + got_b.astype(F32)).astype(BF16)
    far_b = swap(chip_b, "h")

    answer = lax.ppermute(answer, ("y", "z"), [(i - 1, i) for i in range(1, run_count)])
    attended = jnp.concatenate([answer[:STRETCH], attended], axis=0)
    grad_queries = jnp.concatenate([answer[STRETCH:], grad_queries], axis=0)

    groups = lax.axis_size("x") * lax.axis_size("y")
    depth = lax.axis_size("z")
    terms = lax.all_to_all(weight_grad, ("x", "y"), 0, 0, tiled=True)
    rows = jnp.sum(terms.reshape(groups, enc_width // groups, 2 * width).astype(F32), axis=0)
    rows = rows.reshape(depth, -1, 2 * width)
    own_rows = rows.shape[1]
    rows = jnp.pad(rows, ((0, 0), (0, 8 - own_rows), (0, 0)))
    rows = lax.all_to_all(rows, "z", 0, 0, tiled=True)
    weight_rows = jnp.sum(rows, axis=0)[:own_rows]

    half_a = (chip_a.astype(F32) + far_a.astype(F32)).astype(BF16)
    half_b = (chip_b.astype(F32) + far_b.astype(F32)).astype(BF16)
    grad_rows = jnp.stack(
        [
            lax.all_gather(half_a, "c", axis=0, tiled=True),
            lax.all_gather(half_b, "c", axis=0, tiled=True),
        ]
    )
    return (
        attended[None],
        grad_queries[None],
        grad_rows[None],
        weight_rows[:, :width],
        weight_rows[:, width:],
    )


def solution(mesh):
    chips = Mesh(np.asarray(mesh.devices).reshape(4, 4, 8, 2, 2), ("x", "y", "z", "h", "c"))
    runs, heads = ("y", "z"), ("h", "c")
    in_specs = (
        P("x", runs, heads),
        P("x", runs, None, None),
        P(None, heads),
        P(None, heads),
        P("x", runs, None),
        P("x", runs),
        P("x", runs, heads),
    )
    out_specs = (
        P("x", runs, heads),
        P("x", runs, heads),
        P("x", runs, None, None),
        P(("x", "y", "z"), heads),
        P(("x", "y", "z"), heads),
    )
    return jax.shard_map(shards, mesh=chips, in_specs=in_specs, out_specs=out_specs, check_vma=False)
```

```python
import functools

import jax
import jax.numpy as jnp
import numpy as np
from jax import lax
from jax.experimental import pallas as pl
from jax.experimental.pallas import tpu as pltpu
from jax.sharding import Mesh, PartitionSpec as P

HEAD_DIM = 128
STRETCH = 64
BF16 = jnp.bfloat16
F32 = jnp.float32

masked_score = -1e30


def matmul(left, right, left_dim, right_dim):
    contracted = (((left_dim,), (right_dim,)), ((), ()))
    return lax.dot_general(left, right, contracted, preferred_element_type=F32)


def project(encodings, weight):
    return matmul(encodings, weight[...], 1, 0).astype(BF16)


def attend(keys_all, values_all, usable, gate, queries, grad_out, out):
    attended, grad_queries, grad_keys, grad_values = out
    score_scale = HEAD_DIM ** (-0.5)
    gated_all = jnp.where(gate, grad_out, jnp.zeros_like(grad_out))
    for head in range(queries.shape[1] // HEAD_DIM):
        span = slice(head * HEAD_DIM, (head + 1) * HEAD_DIM)
        query, grad = queries[:, span], gated_all[:, span]
        keys, values = keys_all[:, span], values_all[:, span]
        scores = jnp.where(usable, matmul(query, keys, 1, 1) * score_scale, masked_score)
        raised = jnp.exp(scores - jnp.max(scores, axis=-1, keepdims=True))
        weights = raised / jnp.sum(raised, axis=-1, keepdims=True)
        weights_half = weights.astype(BF16)
        mixed = matmul(weights_half, values, 1, 0)
        attended[:, span] = jnp.where(gate, mixed, 0.0).astype(BF16)
        grad_weights = matmul(grad, values, 1, 1)
        inner = jnp.sum(weights * grad_weights, axis=-1, keepdims=True)
        grad_scores = (weights * (grad_weights - inner) * score_scale).astype(BF16)
        grad_queries[:, span] = matmul(grad_scores, keys, 1, 0).astype(BF16)
        grad_keys[:, span] = matmul(grad_scores, query, 0, 0).astype(BF16)
        grad_values[:, span] = matmul(weights_half, grad, 0, 0).astype(BF16)


def encoding_partials(core, key_weight, value_weight, grad_keys, grad_values, kept, sent):
    half = kept.shape[0]

    def partial_of(part):
        rows = pl.ds(pl.multiple_of(part * half, half), half)
        return matmul(grad_keys[rows, :], key_weight[...], 1, 1) + matmul(
            grad_values[rows, :], value_weight[...], 1, 1
        )

    sent[...] = partial_of(1 - core).astype(BF16)
    kept[...] = partial_of(core)


def load(documents_in, ids_in, neighbours_in, key_in, value_in, queries_in, grad_in, *rest):
    payload, documents, ids, neighbours, key_weight, value_weight, queries, grad_out, sems = rest
    moves = (
        (documents_in, documents),
        (queries_in.at[0, 0:STRETCH], payload.at[0:STRETCH]),
        (grad_in.at[0, 0:STRETCH], payload.at[STRETCH:2 * STRETCH]),
        (neighbours_in.at[0], neighbours),
        (key_in, key_weight),
        (value_in, value_weight),
        (queries_in.at[0, STRETCH:2 * STRETCH], queries),
        (grad_in.at[0, STRETCH:2 * STRETCH], grad_out),
        (ids_in.at[0], ids),
    )
    copies = [pltpu.make_async_copy(*move, sems.at[i]) for i, move in enumerate(moves)]
    for copy in copies:
        copy.start()
    copies[0].wait()
    first = documents[0:1, 0:1].astype(F32)
    payload[2 * STRETCH:, :] = jnp.broadcast_to(first, (16, payload.shape[1])).astype(BF16)
    for copy in copies[1:]:
        copy.wait()


def own_pair(documents, ids, neighbours, key_weight, value_weight, queries, grad_out, *out):
    attended, grad_queries, grad_keys, grad_values, kept, sent, next_keys, next_values = out
    gate = documents[0:1, 0:1] == documents[0:1, 1:2]
    attend(
        project(neighbours[0], key_weight), project(neighbours[0], value_weight),
        ids[0:1, :] != 0, gate,
        queries[...], grad_out[...], (attended, grad_queries, grad_keys, grad_values),
    )
    encoding_partials(lax.axis_index("c"), key_weight, value_weight, grad_keys, grad_values, kept, sent)
    next_keys[...] = project(neighbours[1], key_weight)
    next_values[...] = project(neighbours[1], value_weight)


def next_pair(
    documents, ids, key_weight, value_weight, keys, values, payload, kept_a, sent_a, *out
):
    answer, grad_keys, grad_values, kept, sent = out
    kept[0] = kept_a[...]
    sent[0] = sent_a[...]
    last_run = lax.axis_size("y") * lax.axis_size("z") - 1
    run = lax.axis_index("y") * lax.axis_size("z") + lax.axis_index("z")
    follows = jnp.full((1, 1), run, jnp.int32) < last_run
    document = payload[2 * STRETCH:2 * STRETCH + 1, 0:1].astype(F32)
    gate = jnp.logical_and(document == documents[0:1, 1:2].astype(F32), follows)
    attend(
        keys[...], values[...], ids[1:2, :] != 0, gate,
        payload[0:STRETCH, :], payload[STRETCH:2 * STRETCH, :],
        (answer.at[0:STRETCH], answer.at[STRETCH:2 * STRETCH], grad_keys, grad_values),
    )
    encoding_partials(lax.axis_index("c"), key_weight, value_weight, grad_keys, grad_values, kept.at[1], sent.at[1])


def weight_partial(neighbours, keys_a, keys_b, values_a, values_b, weight_grad):
    width = keys_a.shape[1]
    for side, (first, second) in enumerate(((keys_a, keys_b), (values_a, values_b))):
        total = matmul(neighbours[0], first[...], 0, 0) + matmul(neighbours[1], second[...], 0, 0)
        weight_grad[:, side * width:(side + 1) * width] = total.astype(BF16)


def join(weight_rows, answer, second_attended, second_queries, attended, grad_queries):
    attended[0, 0:STRETCH, :] = answer[0:STRETCH, :]
    attended[0, STRETCH:, :] = second_attended[...]
    grad_queries[0, 0:STRETCH, :] = answer[STRETCH:, :]
    grad_queries[0, STRETCH:, :] = second_queries[...]


def add_cores(kept, got, weight_grad, chip_sum):
    chip_sum[...] = (kept[...] + got[...].astype(F32)).astype(BF16)


def finish(near, far, weight_rows, halves):
    halves[...] = (near[...].astype(F32) + far[...].astype(F32)).astype(BF16)


def call(kernel, out_shapes, flops, moved, space=pltpu.VMEM, scratch=()):
    def run(*arrays):
        if space == pltpu.HBM:
            arrays = [pltpu.with_memory_space_constraint(a, pltpu.HBM) for a in arrays]
        return pl.pallas_call(
            kernel,
            out_shape=[jax.ShapeDtypeStruct(s, d) for s, d in out_shapes],
            in_specs=[pl.BlockSpec(memory_space=space)] * len(arrays),
            out_specs=[pl.BlockSpec(memory_space=pltpu.VMEM)] * len(out_shapes),
            scratch_shapes=list(scratch),
            compiler_params=pltpu.CompilerParams(vmem_limit_bytes=48 * 2**20),
            cost_estimate=pl.CostEstimate(flops=flops, bytes_accessed=moved, transcendentals=0),
        )(*arrays)

    return run


def swap(block, axis):
    return lax.ppermute(block, axis, [(0, 1), (1, 0)])


def scatter_sum(rows, axis):
    index = lax.axis_index(axis)
    count = lax.axis_size(axis)
    step = 1
    while step < count:
        pairs = rows.reshape(rows.shape[0] // 2, 2, *rows.shape[1:])
        upper = (index // step) % 2 == 1
        sent = jnp.where(upper, pairs[:, 0], pairs[:, 1])
        kept = jnp.where(upper, pairs[:, 1], pairs[:, 0])
        rows = kept + lax.ppermute(sent, axis, [(i, i ^ step) for i in range(count)])
        step *= 2
    return rows[0]


def shards(queries, neighbours, key_weight, value_weight, neighbour_ids, block_document, grad_out):
    tokens, width = queries.shape[1:]
    slots, enc_width = neighbours.shape[2:]
    half = slots // 2
    run_count = lax.axis_size("y") * lax.axis_size("z")
    half_rows = [((half, enc_width), F32), ((half, enc_width), BF16)]
    payload, documents, ids, encodings, key_local, value_local, second_queries, second_grad = call(
        load,
        [
            ((2 * STRETCH + 16, width), BF16),
            (block_document.shape, jnp.int32),
            (neighbour_ids.shape[1:], jnp.int32),
            (neighbours.shape[1:], BF16),
            (key_weight.shape, BF16),
            (value_weight.shape, BF16),
            ((STRETCH, width), BF16),
            ((STRETCH, width), BF16),
        ],
        0,
        6_000_000,
        space=pltpu.HBM,
        scratch=[pltpu.SemaphoreType.DMA((9,))],
    )(block_document, neighbour_ids, neighbours, key_weight, value_weight, queries, grad_out)
    payload = lax.ppermute(payload, ("y", "z"), [(i, i - 1) for i in range(1, run_count)])

    attended, grad_queries, keys_a, values_a, kept_a, sent_a, next_keys, next_values = call(
        own_pair,
        [((STRETCH, width), BF16)] * 2
        + [((slots, width), BF16)] * 2
        + half_rows
        + [((slots, width), BF16)] * 2,
        1_100_000_000,
        10_000_000,
    )(documents, ids, encodings, key_local, value_local, second_queries, second_grad)

    answer, keys_b, values_b, kept, sent = call(
        next_pair,
        [((2 * STRETCH, width), BF16)]
        + [((slots, width), BF16)] * 2
        + [((2, half, enc_width), F32), ((2, half, enc_width), BF16)],
        1_100_000_000,
        10_000_000,
    )(
        documents, ids, key_local, value_local, next_keys, next_values, payload, kept_a, sent_a
    )
    got = swap(sent, "c")

    (weight_grad,) = call(
        weight_partial, [((enc_width, 2 * width), BF16)], 940_000_000, 6_000_000
    )(encodings, keys_a, keys_b, values_a, values_b)
    groups = lax.axis_size("x") * lax.axis_size("y")
    depth = lax.axis_size("z")
    (chip_sum,) = call(add_cores, [((2, half, enc_width), BF16)], 1_000_000, 2_000_000)(
        kept, got, weight_grad
    )
    far_sum = swap(chip_sum, "h")
    def sum_over_rows(partial):
        terms = lax.all_to_all(partial, ("x", "y"), 0, 0, tiled=True)
        rows = jnp.sum(terms.reshape(groups, enc_width // groups, 2 * width).astype(F32), axis=0)
        rows = rows.reshape(depth, -1, 2 * width)
        return jnp.pad(rows, ((0, 0), (0, 8 - rows.shape[1]), (0, 0))).astype(BF16)

    def sum_over_depth(rows):
        rows = lax.all_to_all(rows, "z", 0, 0, tiled=True)
        return jnp.sum(rows.astype(F32), axis=0)

    always = block_document[0, 0] >= 0
    rows = lax.cond(
        always,
        sum_over_rows,
        lambda partial: jnp.zeros((depth, 8, 2 * width), BF16),
        weight_grad,
    )
    answer, rows = lax.optimization_barrier((answer, rows))
    answer = lax.ppermute(answer, ("y", "z"), [(i - 1, i) for i in range(1, run_count)])
    weight_rows = lax.cond(
        always, sum_over_depth, lambda rows: jnp.zeros(rows.shape[1:], F32), rows
    )
    attended, grad_queries = call(join, [((1, tokens, width), BF16)] * 2, 1_000_000, 1_000_000)(
        weight_rows, answer, attended, grad_queries
    )

    (halves,) = call(finish, [((2, half, enc_width), BF16)], 1_000_000, 1_000_000)(
        chip_sum, far_sum, weight_rows
    )
    grad_rows = lax.all_gather(halves, "c", axis=1, tiled=True)
    weight_rows = weight_rows[:enc_width // groups // depth]
    return (
        attended,
        grad_queries,
        grad_rows[None],
        weight_rows[:, :width],
        weight_rows[:, width:],
    )


def solution(mesh):
    chips = Mesh(np.asarray(mesh.devices).reshape(4, 4, 8, 2, 2), ("x", "y", "z", "h", "c"))
    runs, heads = ("y", "z"), ("h", "c")
    in_specs = (
        P("x", runs, heads),
        P("x", runs, None, None),
        P(None, heads),
        P(None, heads),
        P("x", runs, None),
        P("x", runs),
        P("x", runs, heads),
    )
    out_specs = (
        P("x", runs, heads),
        P("x", runs, heads),
        P("x", runs, None, None),
        P(("x", "y", "z"), heads),
        P(("x", "y", "z"), heads),
    )
    return jax.shard_map(shards, mesh=chips, in_specs=in_specs, out_specs=out_specs, check_vma=False)
```

```python
import functools

import jax
import jax.numpy as jnp
import numpy as np
from jax import lax
from jax.experimental import pallas as pl
from jax.experimental.pallas import tpu as pltpu
from jax.sharding import Mesh, PartitionSpec as P

HEAD_DIM = 128
STRETCH = 64
BF16 = jnp.bfloat16
F32 = jnp.float32

masked_score = -1e30


def matmul(left, right, left_dim, right_dim):
    contracted = (((left_dim,), (right_dim,)), ((), ()))
    return lax.dot_general(left, right, contracted, preferred_element_type=F32)


def project(encodings, weight):
    return matmul(encodings, weight[...], 1, 0).astype(BF16)


def attend(keys_all, values_all, usable, gate, queries, grad_out, out):
    attended, grad_queries, grad_keys, grad_values = out
    score_scale = HEAD_DIM ** (-0.5)
    gated_all = jnp.where(gate, grad_out, jnp.zeros_like(grad_out))
    for head in range(queries.shape[1] // HEAD_DIM):
        span = slice(head * HEAD_DIM, (head + 1) * HEAD_DIM)
        query, grad = queries[:, span], gated_all[:, span]
        keys, values = keys_all[:, span], values_all[:, span]
        scores = jnp.where(usable, matmul(query, keys, 1, 1) * score_scale, masked_score)
        raised = jnp.exp(scores - jnp.max(scores, axis=-1, keepdims=True))
        weights = raised / jnp.sum(raised, axis=-1, keepdims=True)
        weights_half = weights.astype(BF16)
        mixed = matmul(weights_half, values, 1, 0)
        attended[:, span] = jnp.where(gate, mixed, 0.0).astype(BF16)
        grad_weights = matmul(grad, values, 1, 1)
        inner = jnp.sum(weights * grad_weights, axis=-1, keepdims=True)
        grad_scores = (weights * (grad_weights - inner) * score_scale).astype(BF16)
        grad_queries[:, span] = matmul(grad_scores, keys, 1, 0).astype(BF16)
        grad_keys[:, span] = matmul(grad_scores, query, 0, 0).astype(BF16)
        grad_values[:, span] = matmul(weights_half, grad, 0, 0).astype(BF16)


def encoding_partials(core, key_weight, value_weight, grad_keys, grad_values, kept, sent):
    half = kept.shape[0]

    def partial_of(part):
        rows = pl.ds(pl.multiple_of(part * half, half), half)
        return matmul(grad_keys[rows, :], key_weight[...], 1, 1) + matmul(
            grad_values[rows, :], value_weight[...], 1, 1
        )

    sent[...] = partial_of(1 - core).astype(BF16)
    kept[...] = partial_of(core)


def copy_all(moves, sems):
    copies = [pltpu.make_async_copy(*move, sems.at[i]) for i, move in enumerate(moves)]
    for copy in copies:
        copy.start()
    return copies


def pack(documents_in, queries_in, grad_in, payload, documents, sems):
    copies = copy_all(
        (
            (documents_in, documents),
            (queries_in.at[0, 0:STRETCH], payload.at[0:STRETCH]),
            (grad_in.at[0, 0:STRETCH], payload.at[STRETCH:2 * STRETCH]),
        ),
        sems,
    )
    copies[0].wait()
    first = documents[0:1, 0:1].astype(F32)
    payload[2 * STRETCH:, :] = jnp.broadcast_to(first, (16, payload.shape[1])).astype(BF16)
    for copy in copies[1:]:
        copy.wait()


def load(ids_in, neighbours_in, key_in, value_in, queries_in, grad_in, *rest):
    ids, neighbours, key_weight, value_weight, queries, grad_out, sems = rest
    copies = copy_all(
        (
            (neighbours_in.at[0], neighbours),
            (key_in, key_weight),
            (value_in, value_weight),
            (queries_in.at[0, STRETCH:2 * STRETCH], queries),
            (grad_in.at[0, STRETCH:2 * STRETCH], grad_out),
            (ids_in.at[0], ids),
        ),
        sems,
    )
    for copy in copies:
        copy.wait()


def own_pair(documents, ids, neighbours, key_weight, value_weight, queries, grad_out, *out):
    attended, grad_queries, grad_keys, grad_values, kept, sent, next_keys, next_values = out
    gate = documents[0:1, 0:1] == documents[0:1, 1:2]
    attend(
        project(neighbours[0], key_weight), project(neighbours[0], value_weight),
        ids[0:1, :] != 0, gate,
        queries[...], grad_out[...], (attended, grad_queries, grad_keys, grad_values),
    )
    encoding_partials(lax.axis_index("c"), key_weight, value_weight, grad_keys, grad_values, kept, sent)
    next_keys[...] = project(neighbours[1], key_weight)
    next_values[...] = project(neighbours[1], value_weight)


def next_pair(
    documents, ids, key_weight, value_weight, keys, values, payload, kept_a, sent_a, *out
):
    answer, grad_keys, grad_values, kept, sent = out
    kept[0] = kept_a[...]
    sent[0] = sent_a[...]
    last_run = lax.axis_size("y") * lax.axis_size("z") - 1
    run = lax.axis_index("y") * lax.axis_size("z") + lax.axis_index("z")
    follows = jnp.full((1, 1), run, jnp.int32) < last_run
    document = payload[2 * STRETCH:2 * STRETCH + 1, 0:1].astype(F32)
    gate = jnp.logical_and(document == documents[0:1, 1:2].astype(F32), follows)
    attend(
        keys[...], values[...], ids[1:2, :] != 0, gate,
        payload[0:STRETCH, :], payload[STRETCH:2 * STRETCH, :],
        (answer.at[0:STRETCH], answer.at[STRETCH:2 * STRETCH], grad_keys, grad_values),
    )
    encoding_partials(lax.axis_index("c"), key_weight, value_weight, grad_keys, grad_values, kept.at[1], sent.at[1])


def weight_partial(neighbours, keys_a, keys_b, values_a, values_b, weight_grad):
    width = keys_a.shape[1]
    for side, (first, second) in enumerate(((keys_a, keys_b), (values_a, values_b))):
        total = matmul(neighbours[0], first[...], 0, 0) + matmul(neighbours[1], second[...], 0, 0)
        weight_grad[:, side * width:(side + 1) * width] = total.astype(BF16)


def join(answer, second_attended, second_queries, attended, grad_queries):
    attended[0, 0:STRETCH, :] = answer[0:STRETCH, :]
    attended[0, STRETCH:, :] = second_attended[...]
    grad_queries[0, 0:STRETCH, :] = answer[STRETCH:, :]
    grad_queries[0, STRETCH:, :] = second_queries[...]


def add_cores(kept, got, weight_grad, chip_sum):
    chip_sum[...] = (kept[...] + got[...].astype(F32)).astype(BF16)


def finish(near, far, rows, attended, halves):
    halves[...] = (near[...].astype(F32) + far[...].astype(F32)).astype(BF16)


def call(kernel, out_shapes, flops, moved, space=pltpu.VMEM, scratch=()):
    def run(*arrays):
        if space == pltpu.HBM:
            arrays = [pltpu.with_memory_space_constraint(a, pltpu.HBM) for a in arrays]
        return pl.pallas_call(
            kernel,
            out_shape=[jax.ShapeDtypeStruct(s, d) for s, d in out_shapes],
            in_specs=[pl.BlockSpec(memory_space=space)] * len(arrays),
            out_specs=[pl.BlockSpec(memory_space=pltpu.VMEM)] * len(out_shapes),
            scratch_shapes=list(scratch),
            compiler_params=pltpu.CompilerParams(vmem_limit_bytes=48 * 2**20),
            cost_estimate=pl.CostEstimate(flops=flops, bytes_accessed=moved, transcendentals=0),
        )(*arrays)

    return run


def swap(block, axis):
    return lax.ppermute(block, axis, [(0, 1), (1, 0)])


def scatter_sum(rows, axis):
    index = lax.axis_index(axis)
    count = lax.axis_size(axis)
    step = 1
    while step < count:
        pairs = rows.reshape(rows.shape[0] // 2, 2, *rows.shape[1:])
        upper = (index // step) % 2 == 1
        sent = jnp.where(upper, pairs[:, 0], pairs[:, 1])
        kept = jnp.where(upper, pairs[:, 1], pairs[:, 0])
        rows = kept + lax.ppermute(sent, axis, [(i, i ^ step) for i in range(count)])
        step *= 2
    return rows[0]


def shards(queries, neighbours, key_weight, value_weight, neighbour_ids, block_document, grad_out):
    tokens, width = queries.shape[1:]
    slots, enc_width = neighbours.shape[2:]
    half = slots // 2
    run_count = lax.axis_size("y") * lax.axis_size("z")
    half_rows = [((half, enc_width), F32), ((half, enc_width), BF16)]
    payload, documents = call(
        pack,
        [((2 * STRETCH + 16, width), BF16), (block_document.shape, jnp.int32)],
        0,
        300_000,
        space=pltpu.HBM,
        scratch=[pltpu.SemaphoreType.DMA((3,))],
    )(block_document, queries, grad_out)
    payload = lax.ppermute(payload, ("y", "z"), [(i, i - 1) for i in range(1, run_count)])
    ids, encodings, key_local, value_local, second_queries, second_grad = call(
        load,
        [
            (neighbour_ids.shape[1:], jnp.int32),
            (neighbours.shape[1:], BF16),
            (key_weight.shape, BF16),
            (value_weight.shape, BF16),
            ((STRETCH, width), BF16),
            ((STRETCH, width), BF16),
        ],
        0,
        6_000_000,
        space=pltpu.HBM,
        scratch=[pltpu.SemaphoreType.DMA((6,))],
    )(neighbour_ids, neighbours, key_weight, value_weight, queries, grad_out)

    attended, grad_queries, keys_a, values_a, kept_a, sent_a, next_keys, next_values = call(
        own_pair,
        [((STRETCH, width), BF16)] * 2
        + [((slots, width), BF16)] * 2
        + half_rows
        + [((slots, width), BF16)] * 2,
        1_100_000_000,
        10_000_000,
    )(documents, ids, encodings, key_local, value_local, second_queries, second_grad)

    answer, keys_b, values_b, kept, sent = call(
        next_pair,
        [((2 * STRETCH, width), BF16)]
        + [((slots, width), BF16)] * 2
        + [((2, half, enc_width), F32), ((2, half, enc_width), BF16)],
        1_100_000_000,
        10_000_000,
    )(
        documents, ids, key_local, value_local, next_keys, next_values, payload, kept_a, sent_a
    )
    got = swap(sent, "c")

    (weight_grad,) = call(
        weight_partial, [((enc_width, 2 * width), BF16)], 940_000_000, 6_000_000
    )(encodings, keys_a, keys_b, values_a, values_b)
    groups = lax.axis_size("x") * lax.axis_size("y")
    depth = lax.axis_size("z")
    (chip_sum,) = call(add_cores, [((2, half, enc_width), BF16)], 1_000_000, 2_000_000)(
        kept, got, weight_grad
    )
    far_sum = swap(chip_sum, "h")
    def sum_over_rows(partial):
        terms = lax.all_to_all(partial, ("x", "y"), 0, 0, tiled=True)
        rows = jnp.sum(terms.reshape(groups, enc_width // groups, 2 * width).astype(F32), axis=0)
        rows = rows.reshape(depth, -1, 2 * width)
        return jnp.pad(rows, ((0, 0), (0, 8 - rows.shape[1]), (0, 0))).astype(BF16)

    always = block_document[0, 0] >= 0
    rows = lax.cond(
        always,
        sum_over_rows,
        lambda partial: jnp.zeros((depth, 8, 2 * width), BF16),
        weight_grad,
    )
    answer, rows = lax.optimization_barrier((answer, rows))
    answer = lax.ppermute(answer, ("y", "z"), [(i - 1, i) for i in range(1, run_count)])
    weight_rows = lax.all_to_all(rows, "z", 0, 0, tiled=True)
    attended, grad_queries = call(join, [((1, tokens, width), BF16)] * 2, 1_000_000, 1_000_000)(
        answer, attended, grad_queries
    )

    (halves,) = call(finish, [((2, half, enc_width), BF16)], 200_000_000_000, 1_000_000)(
        chip_sum, far_sum, rows, attended
    )
    grad_rows = lax.all_gather(halves, "c", axis=1, tiled=True)
    weight_rows, grad_rows = lax.optimization_barrier((weight_rows, grad_rows))
    weight_rows = jnp.sum(weight_rows.astype(F32), axis=0)
    weight_rows = weight_rows[:enc_width // groups // depth]
    return (
        attended,
        grad_queries,
        grad_rows[None],
        weight_rows[:, :width],
        weight_rows[:, width:],
    )


def solution(mesh):
    chips = Mesh(np.asarray(mesh.devices).reshape(4, 4, 8, 2, 2), ("x", "y", "z", "h", "c"))
    runs, heads = ("y", "z"), ("h", "c")
    in_specs = (
        P("x", runs, heads),
        P("x", runs, None, None),
        P(None, heads),
        P(None, heads),
        P("x", runs, None),
        P("x", runs),
        P("x", runs, heads),
    )
    out_specs = (
        P("x", runs, heads),
        P("x", runs, heads),
        P("x", runs, None, None),
        P(("x", "y", "z"), heads),
        P(("x", "y", "z"), heads),
    )
    return jax.shard_map(shards, mesh=chips, in_specs=in_specs, out_specs=out_specs, check_vma=False)
```

```python
import functools

import jax
import jax.numpy as jnp
import numpy as np
from jax import lax
from jax.experimental import pallas as pl
from jax.experimental.pallas import tpu as pltpu
from jax.sharding import Mesh, PartitionSpec as P

HEAD_DIM = 128
STRETCH = 64
BF16 = jnp.bfloat16
F32 = jnp.float32

masked_score = -1e30


def matmul(left, right, left_dim, right_dim):
    contracted = (((left_dim,), (right_dim,)), ((), ()))
    return lax.dot_general(left, right, contracted, preferred_element_type=F32)


def project(encodings, weight):
    return matmul(encodings, weight[...], 1, 0).astype(BF16)


def attend(keys_all, values_all, usable, gate, queries, grad_out, out):
    attended, grad_queries, grad_keys, grad_values = out
    score_scale = HEAD_DIM ** (-0.5)
    gated_all = jnp.where(gate, grad_out, jnp.zeros_like(grad_out))
    for head in range(queries.shape[1] // HEAD_DIM):
        span = slice(head * HEAD_DIM, (head + 1) * HEAD_DIM)
        query, grad = queries[:, span], gated_all[:, span]
        keys, values = keys_all[:, span], values_all[:, span]
        scores = jnp.where(usable, matmul(query, keys, 1, 1) * score_scale, masked_score)
        raised = jnp.exp(scores - jnp.max(scores, axis=-1, keepdims=True))
        weights = raised / jnp.sum(raised, axis=-1, keepdims=True)
        weights_half = weights.astype(BF16)
        mixed = matmul(weights_half, values, 1, 0)
        attended[:, span] = jnp.where(gate, mixed, 0.0).astype(BF16)
        grad_weights = matmul(grad, values, 1, 1)
        inner = jnp.sum(weights * grad_weights, axis=-1, keepdims=True)
        grad_scores = (weights * (grad_weights - inner) * score_scale).astype(BF16)
        grad_queries[:, span] = matmul(grad_scores, keys, 1, 0).astype(BF16)
        grad_keys[:, span] = matmul(grad_scores, query, 0, 0).astype(BF16)
        grad_values[:, span] = matmul(weights_half, grad, 0, 0).astype(BF16)


def encoding_partials(core, key_weight, value_weight, grad_keys, grad_values, kept, sent):
    half = kept.shape[0]

    def partial_of(part):
        rows = pl.ds(pl.multiple_of(part * half, half), half)
        return matmul(grad_keys[rows, :], key_weight[...], 1, 1) + matmul(
            grad_values[rows, :], value_weight[...], 1, 1
        )

    sent[...] = partial_of(1 - core).astype(BF16)
    kept[...] = partial_of(core)


def copy_all(moves, sems):
    copies = [pltpu.make_async_copy(*move, sems.at[i]) for i, move in enumerate(moves)]
    for copy in copies:
        copy.start()
    return copies


def pack(documents_in, queries_in, grad_in, payload, documents, sems):
    copies = copy_all(
        (
            (documents_in, documents),
            (queries_in.at[0, 0:STRETCH], payload.at[0:STRETCH]),
            (grad_in.at[0, 0:STRETCH], payload.at[STRETCH:2 * STRETCH]),
        ),
        sems,
    )
    copies[0].wait()
    first = documents[0:1, 0:1].astype(F32)
    payload[2 * STRETCH:, :] = jnp.broadcast_to(first, (16, payload.shape[1])).astype(BF16)
    for copy in copies[1:]:
        copy.wait()


def load(ids_in, neighbours_in, key_in, value_in, queries_in, grad_in, *rest):
    ids, neighbours, key_weight, value_weight, queries, grad_out, sems = rest
    copies = copy_all(
        (
            (neighbours_in.at[0], neighbours),
            (key_in, key_weight),
            (value_in, value_weight),
            (queries_in.at[0, STRETCH:2 * STRETCH], queries),
            (grad_in.at[0, STRETCH:2 * STRETCH], grad_out),
            (ids_in.at[0], ids),
        ),
        sems,
    )
    for copy in copies:
        copy.wait()


def own_pair(documents, ids, neighbours, key_weight, value_weight, queries, grad_out, *out):
    attended, grad_queries, grad_keys, grad_values, kept, sent, next_keys, next_values = out
    gate = documents[0:1, 0:1] == documents[0:1, 1:2]
    attend(
        project(neighbours[0], key_weight), project(neighbours[0], value_weight),
        ids[0:1, :] != 0, gate,
        queries[...], grad_out[...], (attended, grad_queries, grad_keys, grad_values),
    )
    encoding_partials(lax.axis_index("c"), key_weight, value_weight, grad_keys, grad_values, kept, sent)
    next_keys[...] = project(neighbours[1], key_weight)
    next_values[...] = project(neighbours[1], value_weight)


def next_pair(
    documents, ids, key_weight, value_weight, keys, values, payload, kept_a, sent_a, *out
):
    answer, grad_keys, grad_values, kept, sent = out
    kept[0] = kept_a[...]
    sent[0] = sent_a[...]
    last_run = lax.axis_size("y") * lax.axis_size("z") - 1
    run = lax.axis_index("y") * lax.axis_size("z") + lax.axis_index("z")
    follows = jnp.full((1, 1), run, jnp.int32) < last_run
    document = payload[2 * STRETCH:2 * STRETCH + 1, 0:1].astype(F32)
    gate = jnp.logical_and(document == documents[0:1, 1:2].astype(F32), follows)
    attend(
        keys[...], values[...], ids[1:2, :] != 0, gate,
        payload[0:STRETCH, :], payload[STRETCH:2 * STRETCH, :],
        (answer.at[0:STRETCH], answer.at[STRETCH:2 * STRETCH], grad_keys, grad_values),
    )
    encoding_partials(lax.axis_index("c"), key_weight, value_weight, grad_keys, grad_values, kept.at[1], sent.at[1])


def weight_partial(neighbours, keys_a, keys_b, values_a, values_b, weight_grad):
    width = keys_a.shape[1]
    for side, (first, second) in enumerate(((keys_a, keys_b), (values_a, values_b))):
        total = matmul(neighbours[0], first[...], 0, 0) + matmul(neighbours[1], second[...], 0, 0)
        weight_grad[:, side * width:(side + 1) * width] = total.astype(BF16)


def add_cores(kept, got, weight_grad, chip_sum):
    chip_sum[...] = (kept[...] + got[...].astype(F32)).astype(BF16)


def finish(near, far, rows, answer, second_attended, second_queries, *out):
    halves, attended, grad_queries = out
    halves[...] = (near[...].astype(F32) + far[...].astype(F32)).astype(BF16)
    attended[0, 0:STRETCH, :] = answer[0:STRETCH, :]
    attended[0, STRETCH:, :] = second_attended[...]
    grad_queries[0, 0:STRETCH, :] = answer[STRETCH:, :]
    grad_queries[0, STRETCH:, :] = second_queries[...]


def sum_depth(terms, rows_in, key_grad, value_grad, rows_out):
    rows_out[0] = rows_in[...]
    total = terms[0].astype(F32)
    for part in range(1, terms.shape[0]):
        total += terms[part].astype(F32)
    own, width = key_grad.shape
    key_grad[...] = total[0:own, 0:width]
    value_grad[...] = total[0:own, width:]


def call(kernel, out_shapes, flops, moved, space=pltpu.VMEM, scratch=()):
    def run(*arrays):
        if space == pltpu.HBM:
            arrays = [pltpu.with_memory_space_constraint(a, pltpu.HBM) for a in arrays]
        return pl.pallas_call(
            kernel,
            out_shape=[jax.ShapeDtypeStruct(s, d) for s, d in out_shapes],
            in_specs=[pl.BlockSpec(memory_space=space)] * len(arrays),
            out_specs=[pl.BlockSpec(memory_space=pltpu.VMEM)] * len(out_shapes),
            scratch_shapes=list(scratch),
            compiler_params=pltpu.CompilerParams(vmem_limit_bytes=48 * 2**20),
            cost_estimate=pl.CostEstimate(flops=flops, bytes_accessed=moved, transcendentals=0),
        )(*arrays)

    return run


def swap(block, axis):
    return lax.ppermute(block, axis, [(0, 1), (1, 0)])


def scatter_sum(rows, axis):
    index = lax.axis_index(axis)
    count = lax.axis_size(axis)
    step = 1
    while step < count:
        pairs = rows.reshape(rows.shape[0] // 2, 2, *rows.shape[1:])
        upper = (index // step) % 2 == 1
        sent = jnp.where(upper, pairs[:, 0], pairs[:, 1])
        kept = jnp.where(upper, pairs[:, 1], pairs[:, 0])
        rows = kept + lax.ppermute(sent, axis, [(i, i ^ step) for i in range(count)])
        step *= 2
    return rows[0]


def shards(queries, neighbours, key_weight, value_weight, neighbour_ids, block_document, grad_out):
    tokens, width = queries.shape[1:]
    slots, enc_width = neighbours.shape[2:]
    half = slots // 2
    run_count = lax.axis_size("y") * lax.axis_size("z")
    half_rows = [((half, enc_width), F32), ((half, enc_width), BF16)]
    payload, documents = call(
        pack,
        [((2 * STRETCH + 16, width), BF16), (block_document.shape, jnp.int32)],
        0,
        300_000,
        space=pltpu.HBM,
        scratch=[pltpu.SemaphoreType.DMA((3,))],
    )(block_document, queries, grad_out)
    payload = lax.ppermute(payload, ("y", "z"), [(i, i - 1) for i in range(1, run_count)])
    ids, encodings, key_local, value_local, second_queries, second_grad = call(
        load,
        [
            (neighbour_ids.shape[1:], jnp.int32),
            (neighbours.shape[1:], BF16),
            (key_weight.shape, BF16),
            (value_weight.shape, BF16),
            ((STRETCH, width), BF16),
            ((STRETCH, width), BF16),
        ],
        0,
        6_000_000,
        space=pltpu.HBM,
        scratch=[pltpu.SemaphoreType.DMA((6,))],
    )(neighbour_ids, neighbours, key_weight, value_weight, queries, grad_out)

    attended, grad_queries, keys_a, values_a, kept_a, sent_a, next_keys, next_values = call(
        own_pair,
        [((STRETCH, width), BF16)] * 2
        + [((slots, width), BF16)] * 2
        + half_rows
        + [((slots, width), BF16)] * 2,
        1_100_000_000,
        10_000_000,
    )(documents, ids, encodings, key_local, value_local, second_queries, second_grad)

    answer, keys_b, values_b, kept, sent = call(
        next_pair,
        [((2 * STRETCH, width), BF16)]
        + [((slots, width), BF16)] * 2
        + [((2, half, enc_width), F32), ((2, half, enc_width), BF16)],
        1_100_000_000,
        10_000_000,
    )(
        documents, ids, key_local, value_local, next_keys, next_values, payload, kept_a, sent_a
    )
    got = swap(sent, "c")

    (weight_grad,) = call(
        weight_partial, [((enc_width, 2 * width), BF16)], 940_000_000, 6_000_000
    )(encodings, keys_a, keys_b, values_a, values_b)
    groups = lax.axis_size("x") * lax.axis_size("y")
    depth = lax.axis_size("z")
    (chip_sum,) = call(add_cores, [((2, half, enc_width), BF16)], 1_000_000, 2_000_000)(
        kept, got, weight_grad
    )
    far_sum = swap(chip_sum, "h")
    def sum_over_rows(partial):
        terms = lax.all_to_all(partial, ("x", "y"), 0, 0, tiled=True)
        rows = jnp.sum(terms.reshape(groups, enc_width // groups, 2 * width).astype(F32), axis=0)
        rows = rows.reshape(depth, -1, 2 * width)
        return jnp.pad(rows, ((0, 0), (0, 8 - rows.shape[1]), (0, 0))).astype(BF16)

    always = block_document[0, 0] >= 0
    rows = lax.cond(
        always,
        sum_over_rows,
        lambda partial: jnp.zeros((depth, 8, 2 * width), BF16),
        weight_grad,
    )
    answer, rows = lax.optimization_barrier((answer, rows))
    answer = lax.ppermute(answer, ("y", "z"), [(i - 1, i) for i in range(1, run_count)])
    weight_rows = lax.all_to_all(rows, "z", 0, 0, tiled=True)
    halves, attended, grad_queries = call(
        finish,
        [((2, half, enc_width), BF16)] + [((1, tokens, width), BF16)] * 2,
        200_000_000_000,
        1_000_000,
    )(chip_sum, far_sum, rows, answer, attended, grad_queries)
    grad_rows = lax.all_gather(halves, "c", axis=1, tiled=True)
    key_grad, value_grad, grad_rows = call(
        sum_depth,
        [((enc_width // groups // depth, width), F32)] * 2 + [(neighbours.shape, BF16)],
        1_000_000,
        2_000_000,
    )(weight_rows, grad_rows)
    return attended, grad_queries, grad_rows, key_grad, value_grad


def solution(mesh):
    chips = Mesh(np.asarray(mesh.devices).reshape(4, 4, 8, 2, 2), ("x", "y", "z", "h", "c"))
    runs, heads = ("y", "z"), ("h", "c")
    in_specs = (
        P("x", runs, heads),
        P("x", runs, None, None),
        P(None, heads),
        P(None, heads),
        P("x", runs, None),
        P("x", runs),
        P("x", runs, heads),
    )
    out_specs = (
        P("x", runs, heads),
        P("x", runs, heads),
        P("x", runs, None, None),
        P(("x", "y", "z"), heads),
        P(("x", "y", "z"), heads),
    )
    return jax.shard_map(shards, mesh=chips, in_specs=in_specs, out_specs=out_specs, check_vma=False)
```

```python
import functools

import jax
import jax.numpy as jnp
import numpy as np
from jax import lax
from jax.experimental import pallas as pl
from jax.experimental.pallas import tpu as pltpu
from jax.sharding import Mesh, PartitionSpec as P

HEAD_DIM = 128
STRETCH = 64
BF16 = jnp.bfloat16
F32 = jnp.float32

masked_score = -1e30


def matmul(left, right, left_dim, right_dim):
    contracted = (((left_dim,), (right_dim,)), ((), ()))
    return lax.dot_general(left, right, contracted, preferred_element_type=F32)


def project(encodings, weight):
    return matmul(encodings, weight[...], 1, 0).astype(BF16)


def attend(keys_all, values_all, usable, gate, queries, grad_out, out):
    attended, grad_queries, grad_keys, grad_values = out
    score_scale = HEAD_DIM ** (-0.5)
    gated_all = jnp.where(gate, grad_out, jnp.zeros_like(grad_out))
    for head in range(queries.shape[1] // HEAD_DIM):
        span = slice(head * HEAD_DIM, (head + 1) * HEAD_DIM)
        query, grad = queries[:, span], gated_all[:, span]
        keys, values = keys_all[:, span], values_all[:, span]
        scores = jnp.where(usable, matmul(query, keys, 1, 1) * score_scale, masked_score)
        raised = jnp.exp(scores - jnp.max(scores, axis=-1, keepdims=True))
        weights = raised / jnp.sum(raised, axis=-1, keepdims=True)
        weights_half = weights.astype(BF16)
        mixed = matmul(weights_half, values, 1, 0)
        attended[:, span] = jnp.where(gate, mixed, 0.0).astype(BF16)
        grad_weights = matmul(grad, values, 1, 1)
        inner = jnp.sum(weights * grad_weights, axis=-1, keepdims=True)
        grad_scores = (weights * (grad_weights - inner) * score_scale).astype(BF16)
        grad_queries[:, span] = matmul(grad_scores, keys, 1, 0).astype(BF16)
        grad_keys[:, span] = matmul(grad_scores, query, 0, 0).astype(BF16)
        grad_values[:, span] = matmul(weights_half, grad, 0, 0).astype(BF16)


def rows_partial(part, key_weight, value_weight, grad_keys, grad_values, half):
    rows = pl.ds(pl.multiple_of(part * half, half), half)
    return matmul(grad_keys[rows, :], key_weight[...], 1, 1) + matmul(
        grad_values[rows, :], value_weight[...], 1, 1
    )


def copy_all(moves, sems):
    copies = [pltpu.make_async_copy(*move, sems.at[i]) for i, move in enumerate(moves)]
    for copy in copies:
        copy.start()
    return copies


def pack(documents_in, queries_in, grad_in, payload, documents, sems):
    copies = copy_all(
        (
            (documents_in, documents),
            (queries_in.at[0, 0:STRETCH], payload.at[0:STRETCH]),
            (grad_in.at[0, 0:STRETCH], payload.at[STRETCH:2 * STRETCH]),
        ),
        sems,
    )
    copies[0].wait()
    first = documents[0:1, 0:1].astype(F32)
    payload[2 * STRETCH:, :] = jnp.broadcast_to(first, (16, payload.shape[1])).astype(BF16)
    for copy in copies[1:]:
        copy.wait()


def load(ids_in, neighbours_in, key_in, value_in, queries_in, grad_in, *rest):
    ids, neighbours, key_weight, value_weight, queries, grad_out, sems = rest
    copies = copy_all(
        (
            (neighbours_in.at[0], neighbours),
            (key_in, key_weight),
            (value_in, value_weight),
            (queries_in.at[0, STRETCH:2 * STRETCH], queries),
            (grad_in.at[0, STRETCH:2 * STRETCH], grad_out),
            (ids_in.at[0], ids),
        ),
        sems,
    )
    for copy in copies:
        copy.wait()


def own_pair(documents, ids, neighbours, key_weight, value_weight, queries, grad_out, *out):
    attended, grad_queries, grad_keys, grad_values, kept, sent, next_keys, next_values = out
    gate = documents[0:1, 0:1] == documents[0:1, 1:2]
    attend(
        project(neighbours[0], key_weight), project(neighbours[0], value_weight),
        ids[0:1, :] != 0, gate,
        queries[...], grad_out[...], (attended, grad_queries, grad_keys, grad_values),
    )
    core, grads = lax.axis_index("c"), (key_weight, value_weight, grad_keys, grad_values)
    sent[...] = rows_partial(1 - core, *grads, sent.shape[0]).astype(BF16)
    kept[...] = rows_partial(core, *grads, kept.shape[0])
    next_keys[...] = project(neighbours[1], key_weight)
    next_values[...] = project(neighbours[1], value_weight)


def next_pair(
    documents, ids, key_weight, value_weight, keys, values, payload, sent_a, *out
):
    answer, grad_keys, grad_values, sent = out
    sent[0] = sent_a[...]
    last_run = lax.axis_size("y") * lax.axis_size("z") - 1
    run = lax.axis_index("y") * lax.axis_size("z") + lax.axis_index("z")
    follows = jnp.full((1, 1), run, jnp.int32) < last_run
    document = payload[2 * STRETCH:2 * STRETCH + 1, 0:1].astype(F32)
    gate = jnp.logical_and(document == documents[0:1, 1:2].astype(F32), follows)
    attend(
        keys[...], values[...], ids[1:2, :] != 0, gate,
        payload[0:STRETCH, :], payload[STRETCH:2 * STRETCH, :],
        (answer.at[0:STRETCH], answer.at[STRETCH:2 * STRETCH], grad_keys, grad_values),
    )
    other = 1 - lax.axis_index("c")
    partial = rows_partial(other, key_weight, value_weight, grad_keys, grad_values, sent.shape[1])
    sent[1] = partial.astype(BF16)


def weight_partial(
    neighbours, key_weight, value_weight, keys_a, keys_b, values_a, values_b, kept_a,
    weight_grad, kept,
):
    core, half = lax.axis_index("c"), kept.shape[1]
    kept[0] = kept_a[...]
    kept[1] = rows_partial(core, key_weight, value_weight, keys_b, values_b, half)
    width = keys_a.shape[1]
    for side, (first, second) in enumerate(((keys_a, keys_b), (values_a, values_b))):
        total = matmul(neighbours[0], first[...], 0, 0) + matmul(neighbours[1], second[...], 0, 0)
        weight_grad[:, side * width:(side + 1) * width] = total.astype(BF16)


def add_cores(kept, got, weight_grad, chip_sum):
    chip_sum[...] = (kept[...] + got[...].astype(F32)).astype(BF16)


def finish(near, far, rows, answer, second_attended, second_queries, *out):
    halves, attended, grad_queries = out
    halves[...] = (near[...].astype(F32) + far[...].astype(F32)).astype(BF16)
    attended[0, 0:STRETCH, :] = answer[0:STRETCH, :]
    attended[0, STRETCH:, :] = second_attended[...]
    grad_queries[0, 0:STRETCH, :] = answer[STRETCH:, :]
    grad_queries[0, STRETCH:, :] = second_queries[...]


def sum_depth(terms, rows_in, key_grad, value_grad, rows_out):
    rows_out[0] = rows_in[...]
    total = terms[0].astype(F32)
    for part in range(1, terms.shape[0]):
        total += terms[part].astype(F32)
    own, width = key_grad.shape
    key_grad[...] = total[0:own, 0:width]
    value_grad[...] = total[0:own, width:]


def call(kernel, out_shapes, flops, moved, space=pltpu.VMEM, scratch=()):
    def run(*arrays):
        if space == pltpu.HBM:
            arrays = [pltpu.with_memory_space_constraint(a, pltpu.HBM) for a in arrays]
        return pl.pallas_call(
            kernel,
            out_shape=[jax.ShapeDtypeStruct(s, d) for s, d in out_shapes],
            in_specs=[pl.BlockSpec(memory_space=space)] * len(arrays),
            out_specs=[pl.BlockSpec(memory_space=pltpu.VMEM)] * len(out_shapes),
            scratch_shapes=list(scratch),
            compiler_params=pltpu.CompilerParams(vmem_limit_bytes=48 * 2**20),
            cost_estimate=pl.CostEstimate(flops=flops, bytes_accessed=moved, transcendentals=0),
        )(*arrays)

    return run


def swap(block, axis):
    return lax.ppermute(block, axis, [(0, 1), (1, 0)])


def scatter_sum(rows, axis):
    index = lax.axis_index(axis)
    count = lax.axis_size(axis)
    step = 1
    while step < count:
        pairs = rows.reshape(rows.shape[0] // 2, 2, *rows.shape[1:])
        upper = (index // step) % 2 == 1
        sent = jnp.where(upper, pairs[:, 0], pairs[:, 1])
        kept = jnp.where(upper, pairs[:, 1], pairs[:, 0])
        rows = kept + lax.ppermute(sent, axis, [(i, i ^ step) for i in range(count)])
        step *= 2
    return rows[0]


def shards(queries, neighbours, key_weight, value_weight, neighbour_ids, block_document, grad_out):
    tokens, width = queries.shape[1:]
    slots, enc_width = neighbours.shape[2:]
    half = slots // 2
    run_count = lax.axis_size("y") * lax.axis_size("z")
    half_rows = [((half, enc_width), F32), ((half, enc_width), BF16)]
    payload, documents = call(
        pack,
        [((2 * STRETCH + 16, width), BF16), (block_document.shape, jnp.int32)],
        0,
        300_000,
        space=pltpu.HBM,
        scratch=[pltpu.SemaphoreType.DMA((3,))],
    )(block_document, queries, grad_out)
    payload = lax.ppermute(payload, ("y", "z"), [(i, i - 1) for i in range(1, run_count)])
    ids, encodings, key_local, value_local, second_queries, second_grad = call(
        load,
        [
            (neighbour_ids.shape[1:], jnp.int32),
            (neighbours.shape[1:], BF16),
            (key_weight.shape, BF16),
            (value_weight.shape, BF16),
            ((STRETCH, width), BF16),
            ((STRETCH, width), BF16),
        ],
        0,
        6_000_000,
        space=pltpu.HBM,
        scratch=[pltpu.SemaphoreType.DMA((6,))],
    )(neighbour_ids, neighbours, key_weight, value_weight, queries, grad_out)

    attended, grad_queries, keys_a, values_a, kept_a, sent_a, next_keys, next_values = call(
        own_pair,
        [((STRETCH, width), BF16)] * 2
        + [((slots, width), BF16)] * 2
        + half_rows
        + [((slots, width), BF16)] * 2,
        1_100_000_000,
        10_000_000,
    )(documents, ids, encodings, key_local, value_local, second_queries, second_grad)

    answer, keys_b, values_b, sent = call(
        next_pair,
        [((2 * STRETCH, width), BF16)]
        + [((slots, width), BF16)] * 2
        + [((2, half, enc_width), BF16)],
        1_100_000_000,
        10_000_000,
    )(
        documents, ids, key_local, value_local, next_keys, next_values, payload, sent_a
    )
    got = swap(sent, "c")

    weight_grad, kept = call(
        weight_partial,
        [((enc_width, 2 * width), BF16), ((2, half, enc_width), F32)],
        1_180_000_000,
        8_000_000,
    )(encodings, key_local, value_local, keys_a, keys_b, values_a, values_b, kept_a)
    groups = lax.axis_size("x") * lax.axis_size("y")
    depth = lax.axis_size("z")
    (chip_sum,) = call(add_cores, [((2, half, enc_width), BF16)], 1_000_000, 2_000_000)(
        kept, got, weight_grad
    )
    far_sum = swap(chip_sum, "h")
    def sum_over_rows(partial):
        terms = lax.all_to_all(partial, ("x", "y"), 0, 0, tiled=True)
        rows = jnp.sum(terms.reshape(groups, enc_width // groups, 2 * width).astype(F32), axis=0)
        rows = rows.reshape(depth, -1, 2 * width)
        return jnp.pad(rows, ((0, 0), (0, 8 - rows.shape[1]), (0, 0))).astype(BF16)

    always = block_document[0, 0] >= 0
    rows = lax.cond(
        always,
        sum_over_rows,
        lambda partial: jnp.zeros((depth, 8, 2 * width), BF16),
        weight_grad,
    )
    answer, rows = lax.optimization_barrier((answer, rows))
    answer = lax.ppermute(answer, ("y", "z"), [(i - 1, i) for i in range(1, run_count)])
    weight_rows = lax.all_to_all(rows, "z", 0, 0, tiled=True)
    halves, attended, grad_queries = call(
        finish,
        [((2, half, enc_width), BF16)] + [((1, tokens, width), BF16)] * 2,
        200_000_000_000,
        1_000_000,
    )(chip_sum, far_sum, rows, answer, attended, grad_queries)
    grad_rows = lax.all_gather(halves, "c", axis=1, tiled=True)
    key_grad, value_grad, grad_rows = call(
        sum_depth,
        [((enc_width // groups // depth, width), F32)] * 2 + [(neighbours.shape, BF16)],
        1_000_000,
        2_000_000,
    )(weight_rows, grad_rows)
    return attended, grad_queries, grad_rows, key_grad, value_grad


def solution(mesh):
    chips = Mesh(np.asarray(mesh.devices).reshape(4, 4, 8, 2, 2), ("x", "y", "z", "h", "c"))
    runs, heads = ("y", "z"), ("h", "c")
    in_specs = (
        P("x", runs, heads),
        P("x", runs, None, None),
        P(None, heads),
        P(None, heads),
        P("x", runs, None),
        P("x", runs),
        P("x", runs, heads),
    )
    out_specs = (
        P("x", runs, heads),
        P("x", runs, heads),
        P("x", runs, None, None),
        P(("x", "y", "z"), heads),
        P(("x", "y", "z"), heads),
    )
    return jax.shard_map(shards, mesh=chips, in_specs=in_specs, out_specs=out_specs, check_vma=False)
```

```python
import functools

import jax
import jax.numpy as jnp
import numpy as np
from jax import lax
from jax.experimental import pallas as pl
from jax.experimental.pallas import tpu as pltpu
from jax.sharding import Mesh, PartitionSpec as P

HEAD_DIM = 128
STRETCH = 64
BF16 = jnp.bfloat16
F32 = jnp.float32

masked_score = -1e30


def matmul(left, right, left_dim, right_dim):
    contracted = (((left_dim,), (right_dim,)), ((), ()))
    return lax.dot_general(left, right, contracted, preferred_element_type=F32)


def project(encodings, weight):
    return matmul(encodings, weight[...], 1, 0).astype(BF16)


def attend(keys_all, values_all, usable, gate, queries, grad_out, out):
    attended, grad_queries, grad_keys, grad_values = out
    score_scale = HEAD_DIM ** (-0.5)
    gated_all = jnp.where(gate, grad_out, jnp.zeros_like(grad_out))
    for head in range(queries.shape[1] // HEAD_DIM):
        span = slice(head * HEAD_DIM, (head + 1) * HEAD_DIM)
        query, grad = queries[:, span], gated_all[:, span]
        keys, values = keys_all[:, span], values_all[:, span]
        scores = jnp.where(usable, matmul(query, keys, 1, 1) * score_scale, masked_score)
        raised = jnp.exp(scores - jnp.max(scores, axis=-1, keepdims=True))
        weights = raised / jnp.sum(raised, axis=-1, keepdims=True)
        weights_half = weights.astype(BF16)
        mixed = matmul(weights_half, values, 1, 0)
        attended[:, span] = jnp.where(gate, mixed, 0.0).astype(BF16)
        grad_weights = matmul(grad, values, 1, 1)
        inner = jnp.sum(weights * grad_weights, axis=-1, keepdims=True)
        grad_scores = (weights * (grad_weights - inner) * score_scale).astype(BF16)
        grad_queries[:, span] = matmul(grad_scores, keys, 1, 0).astype(BF16)
        grad_keys[:, span] = matmul(grad_scores, query, 0, 0).astype(BF16)
        grad_values[:, span] = matmul(weights_half, grad, 0, 0).astype(BF16)


def rows_partial(part, key_weight, value_weight, grad_keys, grad_values, half):
    rows = pl.ds(pl.multiple_of(part * half, half), half)
    return matmul(grad_keys[rows, :], key_weight[...], 1, 1) + matmul(
        grad_values[rows, :], value_weight[...], 1, 1
    )


def copy_all(moves, sems):
    copies = [pltpu.make_async_copy(*move, sems.at[i]) for i, move in enumerate(moves)]
    for copy in copies:
        copy.start()
    return copies


def pack(documents_in, queries_in, grad_in, payload, documents, sems):
    copies = copy_all(
        (
            (documents_in, documents),
            (queries_in.at[0, 0:STRETCH], payload.at[0:STRETCH]),
            (grad_in.at[0, 0:STRETCH], payload.at[STRETCH:2 * STRETCH]),
        ),
        sems,
    )
    copies[0].wait()
    first = documents[0:1, 0:1].astype(F32)
    payload[2 * STRETCH:, :] = jnp.broadcast_to(first, (16, payload.shape[1])).astype(BF16)
    for copy in copies[1:]:
        copy.wait()


def load(ids_in, neighbours_in, key_in, value_in, queries_in, grad_in, *rest):
    ids, neighbours, key_weight, value_weight, queries, grad_out, sems = rest
    copies = copy_all(
        (
            (neighbours_in.at[0], neighbours),
            (key_in, key_weight),
            (value_in, value_weight),
            (queries_in.at[0, STRETCH:2 * STRETCH], queries),
            (grad_in.at[0, STRETCH:2 * STRETCH], grad_out),
            (ids_in.at[0], ids),
        ),
        sems,
    )
    for copy in copies:
        copy.wait()


def own_pair(documents, ids, neighbours, key_weight, value_weight, queries, grad_out, *out):
    attended, grad_queries, grad_keys, grad_values, kept, sent, next_keys, next_values = out
    gate = documents[0:1, 0:1] == documents[0:1, 1:2]
    attend(
        project(neighbours[0], key_weight), project(neighbours[0], value_weight),
        ids[0:1, :] != 0, gate,
        queries[...], grad_out[...], (attended, grad_queries, grad_keys, grad_values),
    )
    core, grads = lax.axis_index("c"), (key_weight, value_weight, grad_keys, grad_values)
    sent[...] = rows_partial(1 - core, *grads, sent.shape[0]).astype(BF16)
    kept[...] = rows_partial(core, *grads, kept.shape[0])
    next_keys[...] = project(neighbours[1], key_weight)
    next_values[...] = project(neighbours[1], value_weight)


def next_pair(
    documents, ids, key_weight, value_weight, keys, values, payload, sent_a, *out
):
    answer, grad_keys, grad_values, sent = out
    sent[0] = sent_a[...]
    last_run = lax.axis_size("y") * lax.axis_size("z") - 1
    run = lax.axis_index("y") * lax.axis_size("z") + lax.axis_index("z")
    follows = jnp.full((1, 1), run, jnp.int32) < last_run
    document = payload[2 * STRETCH:2 * STRETCH + 1, 0:1].astype(F32)
    gate = jnp.logical_and(document == documents[0:1, 1:2].astype(F32), follows)
    attend(
        keys[...], values[...], ids[1:2, :] != 0, gate,
        payload[0:STRETCH, :], payload[STRETCH:2 * STRETCH, :],
        (answer.at[0:STRETCH], answer.at[STRETCH:2 * STRETCH], grad_keys, grad_values),
    )
    other = 1 - lax.axis_index("c")
    partial = rows_partial(other, key_weight, value_weight, grad_keys, grad_values, sent.shape[1])
    sent[1] = partial.astype(BF16)


def weight_partial(
    neighbours, key_weight, value_weight, keys_a, keys_b, values_a, values_b, kept_a,
    weight_grad, kept,
):
    core, half = lax.axis_index("c"), kept.shape[1]
    kept[0] = kept_a[...]
    kept[1] = rows_partial(core, key_weight, value_weight, keys_b, values_b, half)
    width = keys_a.shape[1]
    for side, (first, second) in enumerate(((keys_a, keys_b), (values_a, values_b))):
        total = matmul(neighbours[0], first[...], 0, 0) + matmul(neighbours[1], second[...], 0, 0)
        weight_grad[:, side * width:(side + 1) * width] = total.astype(BF16)


def add_cores(kept, got, weight_grad, chip_sum):
    chip_sum[...] = (kept[...] + got[...].astype(F32)).astype(BF16)


def finish(near, far, rows, answer, second_attended, second_queries, *out):
    halves, attended, grad_queries = out
    halves[...] = (near[...].astype(F32) + far[...].astype(F32)).astype(BF16)
    attended[0, 0:STRETCH, :] = answer[0:STRETCH, :]
    attended[0, STRETCH:, :] = second_attended[...]
    grad_queries[0, 0:STRETCH, :] = answer[STRETCH:, :]
    grad_queries[0, STRETCH:, :] = second_queries[...]


def sum_depth(terms, rows_in, key_grad, value_grad, rows_out, sem):
    written = pltpu.make_async_copy(rows_in, rows_out.at[0], sem)
    written.start()
    total = terms[0].astype(F32)
    for part in range(1, terms.shape[0]):
        total += terms[part].astype(F32)
    own, width = key_grad.shape
    key_grad[...] = total[0:own, 0:width]
    value_grad[...] = total[0:own, width:]
    written.wait()


def call(kernel, out_shapes, flops, moved, space=pltpu.VMEM, scratch=(), in_hbm=0):
    def run(*arrays):
        if space == pltpu.HBM:
            arrays = [pltpu.with_memory_space_constraint(a, pltpu.HBM) for a in arrays]
        return pl.pallas_call(
            kernel,
            out_shape=[jax.ShapeDtypeStruct(s, d) for s, d in out_shapes],
            in_specs=[pl.BlockSpec(memory_space=space)] * len(arrays),
            out_specs=[pl.BlockSpec(memory_space=pltpu.VMEM)] * (len(out_shapes) - in_hbm)
            + [pl.BlockSpec(memory_space=pltpu.HBM)] * in_hbm,
            scratch_shapes=list(scratch),
            compiler_params=pltpu.CompilerParams(vmem_limit_bytes=48 * 2**20),
            cost_estimate=pl.CostEstimate(flops=flops, bytes_accessed=moved, transcendentals=0),
        )(*arrays)

    return run


def swap(block, axis):
    return lax.ppermute(block, axis, [(0, 1), (1, 0)])


def scatter_sum(rows, axis):
    index = lax.axis_index(axis)
    count = lax.axis_size(axis)
    step = 1
    while step < count:
        pairs = rows.reshape(rows.shape[0] // 2, 2, *rows.shape[1:])
        upper = (index // step) % 2 == 1
        sent = jnp.where(upper, pairs[:, 0], pairs[:, 1])
        kept = jnp.where(upper, pairs[:, 1], pairs[:, 0])
        rows = kept + lax.ppermute(sent, axis, [(i, i ^ step) for i in range(count)])
        step *= 2
    return rows[0]


def shards(queries, neighbours, key_weight, value_weight, neighbour_ids, block_document, grad_out):
    tokens, width = queries.shape[1:]
    slots, enc_width = neighbours.shape[2:]
    half = slots // 2
    run_count = lax.axis_size("y") * lax.axis_size("z")
    half_rows = [((half, enc_width), F32), ((half, enc_width), BF16)]
    payload, documents = call(
        pack,
        [((2 * STRETCH + 16, width), BF16), (block_document.shape, jnp.int32)],
        0,
        300_000,
        space=pltpu.HBM,
        scratch=[pltpu.SemaphoreType.DMA((3,))],
    )(block_document, queries, grad_out)
    payload = lax.ppermute(payload, ("y", "z"), [(i, i - 1) for i in range(1, run_count)])
    ids, encodings, key_local, value_local, second_queries, second_grad = call(
        load,
        [
            (neighbour_ids.shape[1:], jnp.int32),
            (neighbours.shape[1:], BF16),
            (key_weight.shape, BF16),
            (value_weight.shape, BF16),
            ((STRETCH, width), BF16),
            ((STRETCH, width), BF16),
        ],
        0,
        6_000_000,
        space=pltpu.HBM,
        scratch=[pltpu.SemaphoreType.DMA((6,))],
    )(neighbour_ids, neighbours, key_weight, value_weight, queries, grad_out)

    attended, grad_queries, keys_a, values_a, kept_a, sent_a, next_keys, next_values = call(
        own_pair,
        [((STRETCH, width), BF16)] * 2
        + [((slots, width), BF16)] * 2
        + half_rows
        + [((slots, width), BF16)] * 2,
        1_100_000_000,
        10_000_000,
    )(documents, ids, encodings, key_local, value_local, second_queries, second_grad)

    answer, keys_b, values_b, sent = call(
        next_pair,
        [((2 * STRETCH, width), BF16)]
        + [((slots, width), BF16)] * 2
        + [((2, half, enc_width), BF16)],
        1_100_000_000,
        10_000_000,
    )(
        documents, ids, key_local, value_local, next_keys, next_values, payload, sent_a
    )
    got = swap(sent, "c")

    weight_grad, kept = call(
        weight_partial,
        [((enc_width, 2 * width), BF16), ((2, half, enc_width), F32)],
        1_180_000_000,
        8_000_000,
    )(encodings, key_local, value_local, keys_a, keys_b, values_a, values_b, kept_a)
    groups = lax.axis_size("x") * lax.axis_size("y")
    depth = lax.axis_size("z")
    (chip_sum,) = call(add_cores, [((2, half, enc_width), BF16)], 1_000_000, 2_000_000)(
        kept, got, weight_grad
    )
    far_sum = swap(chip_sum, "h")
    def sum_over_rows(partial):
        terms = lax.all_to_all(partial, ("x", "y"), 0, 0, tiled=True)
        rows = jnp.sum(terms.reshape(groups, enc_width // groups, 2 * width).astype(F32), axis=0)
        rows = rows.reshape(depth, -1, 2 * width)
        return jnp.pad(rows, ((0, 0), (0, 8 - rows.shape[1]), (0, 0))).astype(BF16)

    always = block_document[0, 0] >= 0
    rows = lax.cond(
        always,
        sum_over_rows,
        lambda partial: jnp.zeros((depth, 8, 2 * width), BF16),
        weight_grad,
    )
    answer, rows = lax.optimization_barrier((answer, rows))
    answer = lax.ppermute(answer, ("y", "z"), [(i - 1, i) for i in range(1, run_count)])
    weight_rows = lax.all_to_all(rows, "z", 0, 0, tiled=True)
    halves, attended, grad_queries = call(
        finish,
        [((2, half, enc_width), BF16)] + [((1, tokens, width), BF16)] * 2,
        200_000_000_000,
        1_000_000,
    )(chip_sum, far_sum, rows, answer, attended, grad_queries)
    grad_rows = lax.all_gather(halves, "c", axis=1, tiled=True)
    key_grad, value_grad, grad_rows = call(
        sum_depth,
        [((enc_width // groups // depth, width), F32)] * 2 + [(neighbours.shape, BF16)],
        1_000_000,
        2_000_000,
        scratch=[pltpu.SemaphoreType.DMA],
        in_hbm=1,
    )(weight_rows, grad_rows)
    return attended, grad_queries, grad_rows, key_grad, value_grad


def solution(mesh):
    chips = Mesh(np.asarray(mesh.devices).reshape(4, 4, 8, 2, 2), ("x", "y", "z", "h", "c"))
    runs, heads = ("y", "z"), ("h", "c")
    in_specs = (
        P("x", runs, heads),
        P("x", runs, None, None),
        P(None, heads),
        P(None, heads),
        P("x", runs, None),
        P("x", runs),
        P("x", runs, heads),
    )
    out_specs = (
        P("x", runs, heads),
        P("x", runs, heads),
        P("x", runs, None, None),
        P(("x", "y", "z"), heads),
        P(("x", "y", "z"), heads),
    )
    return jax.shard_map(shards, mesh=chips, in_specs=in_specs, out_specs=out_specs, check_vma=False)
```
